32 devices in a mesh: row: 4 (over y, core), col: 2 (over x), page: 4 (over z).
Axes of the slice: x: 2, y: 2, z: 4, core: 2. Of those that a mesh axis runs over, the one named last changes fastest.
Arguments:
- tokens: bfloat16 [16, 512, 2048], P(('row', 'page'), None, 'col'), may hold values from -6 to 6
- lengths: int32 [16], P(('row', 'page')), may hold values from 1 to 512, 2048 in all
- page_slot: int32 [16, 4], P('row'), may hold values from 0 to 15, as said below
- w_query: float32 [2048, 1024], P(('row', 'page'), 'col'), may hold values from -0.125 to 0.125
- w_keyval: float32 [2, 2048, 256], P(None, ('row', 'page')), may hold values from -0.125 to 0.125
- w_out: float32 [1024, 2048], P('col', ('row', 'page')), may hold values from -0.1875 to 0.1875
- w_gateup: float32 [2, 2048, 5120], P(None, ('row', 'page'), 'col'), may hold values from -0.125 to 0.125
- w_down: float32 [5120, 2048], P('col', ('row', 'page')), may hold values from -0.078125 to 0.078125
- attn_gain: float32 [2048], replicated, may hold values from 0.1 to 1.9
- ffn_gain: float32 [2048], replicated, may hold values from 0.1 to 1.9
- query_gain: float32 [64], replicated, may hold values from 0.1 to 1.9
- key_gain: float32 [64], replicated, may hold values from 0.1 to 1.9
Outputs:
- layer_out: bfloat16 [16, 512, 2048], P(('row', 'page'), None, 'col')
- kv_pages: bfloat16 [2, 64, 128, 1024], P(None, ('row', 'page'), None, 'col')
The draws below stay inside these ranges and needn't reach their ends.
Inputs may be any that keep to these rules, and one draw needn't show every extreme that they name: `lengths`: each prompt's real tokens; in every draw some prompt has exactly 512. `page_slot`: within the prompts of one index of row the values are a permutation; page v belongs to index v // 4 of page; the 4 blocks of the prompts of one device send the same number of blocks to each of the 4 indices of page.
All inputs are finite; a program needn't handle non-finite values. No bound on the sum of `lengths` on one device may be relied on, other than what follows from the above.
Results may differ from the reference program's by a relative error of at most 0.012.
Values may be sent and summed in bfloat16 or wider, within the bound.
A program may use at most 128 MiB of HBM per device.

```python
import math
import jax
import jax.numpy as jnp
import numpy as np
from jax import lax

D = 2048
H = 16
KVH = 4
HD = 64
FF = 5120
LEN = 512
PAGE_LEN = 128
PR_DEV = 1
PROMPTS = 16
BLOCKS = 4
N_ROW = 4
N_COL = 2
N_PAGE = 4


def draw_page_slot(key, part):
    per_device = PR_DEV * BLOCKS
    capacity = per_device // N_PAGE

    def one_sender(sender_key):
        owners = jax.random.permutation(sender_key, jnp.arange(per_device, dtype=jnp.int32) % N_PAGE)
        same_owner = owners[:, None] == owners[None, :]
        earlier = jnp.arange(per_device, dtype=jnp.int32)[None, :] < jnp.arange(per_device, dtype=jnp.int32)[:, None]
        order_in = jnp.sum((same_owner & earlier).astype(jnp.int32), axis=1)
        return (owners, order_in)

    def one_perm(owner_key):
        return jax.random.permutation(owner_key, per_device).astype(jnp.int32)

    def one_group(group_key):
        sender_keys = jax.random.split(jax.random.fold_in(group_key, 1), N_PAGE)
        owners, order_in = jax.vmap(one_sender)(sender_keys)
        recv_pos = jnp.arange(N_PAGE, dtype=jnp.int32)[:, None] * capacity + order_in
        owner_keys = jax.random.split(jax.random.fold_in(group_key, 2), N_PAGE)
        slot_perm = jax.vmap(one_perm)(owner_keys)
        return owners * per_device + slot_perm[owners, recv_pos]
    group_keys = jax.random.split(jax.random.fold_in(key, 7), N_ROW)
    slot_table = jax.vmap(one_group)(group_keys)
    return slot_table.reshape(PROMPTS, BLOCKS).astype(jnp.int32)


def shard_levels(stream_key, extent, pieces, low, top_value):
    level, own = 1.0, jax.random.fold_in(stream_key, 6)
    for axis_at, parts in pieces:
        draws = jnp.exp(jax.random.uniform(jax.random.fold_in(own, axis_at), (parts,), jnp.float32, low / len(pieces), top_value / len(pieces)))
        level = level * jnp.repeat(draws, extent[axis_at] // parts).reshape([-1 if axis == axis_at else 1 for axis in range(len(extent))])
    return level


def length_profile(number_of, total, bound, slope):
    weights = [(1 << 20) // math.isqrt(grade ** slope) + 1 for grade in range(2, number_of + 1)]
    spare, counts = total - bound - (number_of - 1), [1] * (number_of - 1)
    while spare > 0:
        movable = [i for i in range(number_of - 1) if counts[i] < bound]
        mass, budget = sum([weights[i] for i in movable]), spare
        for i in movable:
            extra = min(bound - counts[i], max(1, budget * weights[i] // mass), spare)
            counts[i] = counts[i] + extra
            spare = spare - extra
    return np.array([bound] + counts)


def uneven(stream_key, amount, total, limit, lean):
    if amount == 2:
        one = jax.random.randint(stream_key, (), max(1, total - limit), min(limit, total - 1) + 1)
        return jnp.stack([one, total - one])
    sizes = jnp.asarray(length_profile(amount, total, limit, lean), jnp.int32)
    pairs = (amount - 1) // 2
    source_of, taker = sizes[1:1 + 2 * pairs:2], sizes[2:2 + 2 * pairs:2]
    slack = jnp.minimum(source_of - 1, limit - taker)
    passed = jax.random.randint(jax.random.fold_in(stream_key, 1), (pairs,), 0, 1 << 20) % (slack + 1)
    sizes = sizes.at[1:1 + 2 * pairs:2].set(source_of - passed).at[2:2 + 2 * pairs:2].set(taker + passed)
    return sizes[jax.random.permutation(jax.random.fold_in(stream_key, 2), amount)]


def bell_draw(stream_key, extent, scale, reach, shards=(), held_as=jnp.bfloat16):
    values = jax.random.normal(stream_key, extent, jnp.float32) * scale
    if len(shards) > 0:
        values = shard_levels(stream_key, extent, shards, -0.22, 0.18) * values
    return jnp.clip(values, min=-reach, max=reach).astype(held_as)


def setup_inputs(seed: int = 0) -> dict:
    arg_keys = jax.random.split(jax.random.key(seed), 13)
    tokens = bell_draw(arg_keys[0], (PROMPTS, LEN, D), 1.0, 6.0, ((0, 16), (2, 2)))
    lengths = uneven(arg_keys[1], PROMPTS, PROMPTS * LEN // 4, LEN, 2).astype(jnp.int32)
    page_slot = draw_page_slot(jax.random.fold_in(arg_keys[12], 71), 0)
    w_query = bell_draw(arg_keys[3], (D, H * HD), D ** -0.5, 0.125, ((0, 16), (1, 2)), jnp.float32)
    w_keyval = bell_draw(arg_keys[4], (2, D, KVH * HD), D ** -0.5, 0.125, ((1, 16),), jnp.float32)
    w_out = bell_draw(arg_keys[5], (H * HD, D), (H * HD) ** -0.5, 0.1875, ((0, 2), (1, 16)), jnp.float32)
    w_gateup = bell_draw(arg_keys[6], (2, D, FF), D ** -0.5, 0.125, ((1, 16), (2, 2)), jnp.float32)
    w_down = bell_draw(arg_keys[7], (FF, D), FF ** -0.5, 0.078125, ((0, 2), (1, 16)), jnp.float32)
    attn_gain = jnp.clip(1.0 + 0.18 * jax.random.normal(arg_keys[8], (D,), jnp.float32), 0.1, 1.9)
    ffn_gain = jnp.clip(1.0 + 0.18 * jax.random.normal(arg_keys[9], (D,), jnp.float32), 0.1, 1.9)
    query_gain = jnp.clip(1.0 + 0.18 * jax.random.normal(arg_keys[10], (HD,), jnp.float32), 0.1, 1.9)
    key_gain = jnp.clip(1.0 + 0.18 * jax.random.normal(arg_keys[11], (HD,), jnp.float32), 0.1, 1.9)
    return dict(tokens=tokens, lengths=lengths, page_slot=page_slot, w_query=w_query, w_keyval=w_keyval, w_out=w_out, w_gateup=w_gateup, w_down=w_down, attn_gain=attn_gain, ffn_gain=ffn_gain, query_gain=query_gain, key_gain=key_gain)


def normalize(values, norm_gain):
    mean_sq = lax.optimization_barrier(jnp.mean(values * values, axis=-1, keepdims=True))
    return values * lax.rsqrt(mean_sq + 1e-06) * norm_gain

def rotate(values):
    row_count = values.shape[-3]
    head_dim = values.shape[-1]
    half_dim = head_dim // 2
    frequency = 10000.0 ** (-2.0 * jnp.arange(half_dim, dtype=jnp.float32) / head_dim)
    angles = jnp.arange(row_count, dtype=jnp.float32)[:, None] * frequency[None, :]
    cosine = jnp.cos(angles)[:, None, :]
    sine_table = jnp.sin(angles)[:, None, :]
    leading = values[..., :half_dim]
    trailing = values[..., half_dim:]
    return jnp.concatenate([leading * cosine - trailing * sine_table, trailing * cosine + leading * sine_table], axis=-1)

def attend(query_rows, key_rows, value_rows, length):
    row_count = query_rows.shape[0]
    scores = jnp.einsum('qhd,khd->hqk', query_rows.astype(jnp.float32), key_rows.astype(jnp.float32)) * query_rows.shape[2] ** (-0.5)
    positions = jnp.arange(row_count, dtype=jnp.int32)
    seen_keys = (positions[None, :] <= positions[:, None]) & (positions[None, :] < length)
    exp_scores = jnp.where(seen_keys[None], jnp.exp(scores), jnp.zeros_like(scores))
    attn_probs = (exp_scores / lax.optimization_barrier(jnp.sum(exp_scores, axis=-1, keepdims=True))).astype(jnp.bfloat16)
    attended = jnp.einsum('hqk,khd->qhd', attn_probs.astype(jnp.float32), value_rows.astype(jnp.float32))
    live_rows = (positions < length)[:, None, None]
    return jnp.where(live_rows, attended, jnp.zeros_like(attended)).astype(jnp.bfloat16)

def reference(tokens, lengths, page_slot, w_query, w_keyval, w_out, w_gateup, w_down, attn_gain, ffn_gain, query_gain, key_gain):
    query_server = w_query.astype(jnp.bfloat16)
    keyval_server = w_keyval.astype(jnp.bfloat16)
    out_server = w_out.astype(jnp.bfloat16)
    gateup_server = w_gateup.astype(jnp.bfloat16)
    down_server = w_down.astype(jnp.bfloat16)
    kv_index = jnp.arange(H, dtype=jnp.int32) // (H // KVH)
    columns = (kv_index[:, None] * HD + jnp.arange(HD, dtype=jnp.int32)[None, :]).reshape(-1)
    key_server = jnp.take(keyval_server[0], columns, axis=1)
    value_server = jnp.take(keyval_server[1], columns, axis=1)
    group_cols = H // N_COL * HD
    group_units = FF // N_COL

    def one_prompt(packed):
        prompt, length = packed
        attn_in = normalize(prompt.astype(jnp.float32), attn_gain).astype(jnp.bfloat16)
        q_raw = jnp.dot(attn_in, query_server, preferred_element_type=jnp.float32).reshape(LEN, H, HD)
        k_raw = jnp.dot(attn_in, key_server, preferred_element_type=jnp.float32).reshape(LEN, H, HD)
        v_raw = jnp.dot(attn_in, value_server, preferred_element_type=jnp.float32).reshape(LEN, H, HD)
        queries = rotate(normalize(q_raw, query_gain)).astype(jnp.bfloat16)
        keys_rot = rotate(normalize(k_raw, key_gain)).astype(jnp.bfloat16)
        values_in = v_raw.astype(jnp.bfloat16)
        attended = attend(queries, keys_rot, values_in, length).reshape(LEN, H * HD)
        attn_sum = jnp.zeros((LEN, D), jnp.float32)
        for group_num in range(N_COL):
            lower = group_num * group_cols
            term_part = jnp.dot(attended[:, lower:lower + group_cols], out_server[lower:lower + group_cols], preferred_element_type=jnp.float32)
            attn_sum = attn_sum + lax.optimization_barrier(term_part.astype(jnp.bfloat16)).astype(jnp.float32)
        residual = (prompt.astype(jnp.float32) + attn_sum).astype(jnp.bfloat16)
        ffn_in = normalize(residual.astype(jnp.float32), ffn_gain).astype(jnp.bfloat16)
        gate_proj = jnp.dot(ffn_in, gateup_server[0], preferred_element_type=jnp.float32)
        up_proj = jnp.dot(ffn_in, gateup_server[1], preferred_element_type=jnp.float32)
        hidden = (jax.nn.silu(gate_proj) * up_proj).astype(jnp.bfloat16)
        ffn_sum = jnp.zeros((LEN, D), jnp.float32)
        for group_num in range(N_COL):
            lower = group_num * group_units
            term_part = jnp.dot(hidden[:, lower:lower + group_units], down_server[lower:lower + group_units], preferred_element_type=jnp.float32)
            ffn_sum = ffn_sum + lax.optimization_barrier(term_part.astype(jnp.bfloat16)).astype(jnp.float32)
        layer_rows = (residual.astype(jnp.float32) + ffn_sum).astype(jnp.bfloat16)
        live_rows = (jnp.arange(LEN, dtype=jnp.int32) < length)[:, None, None]
        page_keys = jnp.where(live_rows, keys_rot, jnp.zeros_like(keys_rot)).reshape(BLOCKS, PAGE_LEN, H * HD)
        page_values = jnp.where(live_rows, values_in, jnp.zeros_like(values_in)).reshape(BLOCKS, PAGE_LEN, H * HD)
        return (layer_rows, jnp.stack([page_keys, page_values]))
    layer_out, blocks = lax.map(one_prompt, (tokens, lengths))
    group_base = jnp.arange(PROMPTS, dtype=jnp.int32) // (N_PAGE * PR_DEV) * (N_PAGE * PR_DEV * BLOCKS)
    targets = (group_base[:, None] + page_slot.astype(jnp.int32)).reshape(-1).astype(jnp.int32)
    ordered = jnp.transpose(blocks, (1, 0, 2, 3, 4)).reshape(2, PROMPTS * BLOCKS, PAGE_LEN, H * HD)
    kv_pages = jnp.zeros_like(ordered).at[:, targets].set(ordered)
    return (layer_out, kv_pages)
```

```python
import jax
import jax.numpy as jnp
from jax import lax
from jax.experimental.layout import Layout, with_layout_constraint
from jax.sharding import PartitionSpec as P

PAGE_LEN = 128


def normalize(values, norm_gain):
    mean_sq = jnp.mean(values * values, axis=-1, keepdims=True)
    return values * lax.rsqrt(mean_sq + 1e-06) * norm_gain


def rotate(values):
    row_count = values.shape[-3]
    head_dim = values.shape[-1]
    half_dim = head_dim // 2
    frequency = 10000.0 ** (-2.0 * jnp.arange(half_dim, dtype=jnp.float32) / head_dim)
    angles = jnp.arange(row_count, dtype=jnp.float32)[:, None] * frequency[None, :]
    cosine = jnp.cos(angles)[:, None, :]
    sine_table = jnp.sin(angles)[:, None, :]
    leading = values[..., :half_dim]
    trailing = values[..., half_dim:]
    return jnp.concatenate(
        [leading * cosine - trailing * sine_table, trailing * cosine + leading * sine_table],
        axis=-1,
    )


def attend(query_rows, key_rows, value_rows, length):
    kv_count, row_count, group, head_dim = query_rows.shape
    scores = jnp.einsum(
        "gqre,gke->grqk", query_rows, key_rows, preferred_element_type=jnp.float32
    ) * head_dim ** (-0.5)
    positions = jnp.arange(row_count, dtype=jnp.int32)
    seen_keys = (positions[None, :] <= positions[:, None]) & (positions[None, :] < length)
    exp_scores = jnp.where(seen_keys, jnp.exp(scores), 0.0)
    attn_probs = (exp_scores / jnp.sum(exp_scores, axis=-1, keepdims=True)).astype(jnp.bfloat16)
    attended = jnp.einsum(
        "grqk,gke->qgre", attn_probs, value_rows, preferred_element_type=jnp.float32
    )
    live_rows = (positions < length)[:, None, None, None]
    return jnp.where(live_rows, attended, 0.0).astype(jnp.bfloat16)


def gather_col(values, col_count, col_index):
    if col_count != 2:
        return lax.all_gather(values, "col", axis=values.ndim - 1, tiled=True)
    other = lax.ppermute(values, "col", [(0, 1), (1, 0)])
    first = jnp.where(col_index == 0, values, other)
    second = jnp.where(col_index == 0, other, values)
    return jnp.concatenate([first, second], axis=-1)


def gather_rows(piece):
    rows_major = Layout(major_to_minor=(0, 1))
    piece = with_layout_constraint(piece, rows_major)
    full = lax.all_gather(piece, ("row", "page"), axis=0, tiled=True)
    return with_layout_constraint(full, rows_major)


def on_device(
    tokens,
    lengths,
    page_slot,
    w_query,
    w_keyval,
    w_out,
    w_gateup,
    w_down,
    attn_gain,
    ffn_gain,
    query_gain,
    key_gain,
):
    bf16 = jnp.bfloat16
    f32 = jnp.float32
    col_count = lax.axis_size("col")
    col_index = lax.axis_index("col")
    head_dim = query_gain.shape[0]
    local_width = w_query.shape[1]
    local_heads = local_width // head_dim
    kv_heads = w_keyval.shape[2] // head_dim
    group_size = local_heads * col_count // kv_heads
    kv_count = max(1, local_heads // group_size)
    rep = local_heads // kv_count
    kv_width = kv_count * head_dim
    kv_start = (col_index * local_heads // group_size) * head_dim
    prompt_count, seq_len, local_feat = tokens.shape
    model_width = attn_gain.shape[0]
    unit_count = w_gateup.shape[2]

    gathered = gather_col(tokens, col_count, col_index)

    keyval_piece = lax.dynamic_slice_in_dim(w_keyval, kv_start, kv_width, axis=2)
    attn_piece = jnp.concatenate(
        [w_query, keyval_piece[0], keyval_piece[1], w_out.T], axis=1
    ).astype(bf16)
    gateup_piece = jnp.concatenate([w_gateup[0], w_gateup[1]], axis=1).astype(bf16)
    down_piece = w_down.T.astype(bf16)
    attn_full = gather_rows(attn_piece)
    gateup_full = gather_rows(gateup_piece)
    down_full = gather_rows(down_piece)
    qkv_width = local_width + 2 * kv_width
    out_t = attn_full[:, qkv_width:]

    attn_in = normalize(gathered.astype(f32), attn_gain).astype(bf16)
    projected = jnp.dot(
        attn_in.reshape(-1, model_width), attn_full[:, :qkv_width], preferred_element_type=f32
    ).reshape(prompt_count, seq_len, qkv_width)
    heads = projected[:, :, : local_width + kv_width].reshape(
        prompt_count, seq_len, local_heads + kv_count, head_dim
    )
    gains = jnp.concatenate(
        [
            jnp.broadcast_to(query_gain, (local_heads, head_dim)),
            jnp.broadcast_to(key_gain, (kv_count, head_dim)),
        ]
    )
    rotated = rotate(normalize(heads, gains)).astype(bf16)
    values_in = projected[:, :, local_width + kv_width :].astype(bf16)
    keys_rot = rotated[:, :, local_heads:]
    parts = []
    for prompt in range(prompt_count):
        query_rows = rotated[prompt, :, :local_heads].reshape(seq_len, kv_count, rep, head_dim)
        parts.append(
            attend(
                query_rows.transpose(1, 0, 2, 3),
                keys_rot[prompt].transpose(1, 0, 2),
                values_in[prompt].reshape(seq_len, kv_count, head_dim).transpose(1, 0, 2),
                lengths[prompt],
            ).reshape(seq_len, local_width)
        )
    attended = jnp.stack(parts).reshape(-1, local_width)
    attn_terms = lax.dot_general(
        attended, out_t, (((1,), (1,)), ((), ())), preferred_element_type=f32
    ).astype(bf16).reshape(prompt_count, seq_len, model_width)

    if col_count == 2:
        attn_other = lax.ppermute(attn_terms, "col", [(0, 1), (1, 0)])
        attn_sum = attn_terms.astype(f32) + attn_other.astype(f32)
        residual_all = (gathered.astype(f32) + attn_sum).astype(bf16)
        residual = lax.dynamic_slice_in_dim(
            residual_all, col_index * local_feat, local_feat, axis=2
        )
    else:
        attn_sum = lax.psum_scatter(attn_terms, "col", scatter_dimension=2, tiled=True)
        residual = (tokens.astype(f32) + attn_sum.astype(f32)).astype(bf16)
        residual_all = lax.all_gather(residual, "col", axis=2, tiled=True)

    page_count = lax.axis_size("page")
    page_index = lax.axis_index("page")
    blocks_each = prompt_count * (seq_len // PAGE_LEN)
    capacity = blocks_each // page_count
    owners = page_slot // blocks_each
    local_slot = page_slot % blocks_each
    owners = owners.reshape(page_count, blocks_each)
    local_slot = local_slot.reshape(page_count, blocks_each)
    same_owner = owners[:, :, None] == owners[:, None, :]
    earlier = (
        jnp.arange(blocks_each, dtype=jnp.int32)[None, :]
        < jnp.arange(blocks_each, dtype=jnp.int32)[:, None]
    )
    order_in = jnp.sum((same_owner & earlier[None]).astype(jnp.int32), axis=2)
    my_owners = lax.dynamic_index_in_dim(owners, page_index, 0, keepdims=False)
    my_order = lax.dynamic_index_in_dim(order_in, page_index, 0, keepdims=False)
    send_pos = my_owners * capacity + my_order
    live_rows = (jnp.arange(seq_len, dtype=jnp.int32)[None, :] < lengths[:, None])[:, :, None]
    keys_flat = keys_rot.reshape(prompt_count, seq_len, kv_width)
    both = jnp.stack([keys_flat, values_in])
    both = jnp.where(live_rows[None], both, jnp.zeros_like(both)).reshape(
        2, blocks_each, PAGE_LEN, kv_width
    )
    from_block = jnp.argmax(
        send_pos[None, :] == jnp.arange(blocks_each, dtype=jnp.int32)[:, None], axis=1
    )
    outgoing = jnp.take(both, from_block, axis=1)
    incoming = lax.all_to_all(outgoing, "page", split_axis=1, concat_axis=1, tiled=True)
    arrival_hit = (owners[:, None, :] == page_index) & (
        order_in[:, None, :] == jnp.arange(capacity, dtype=jnp.int32)[None, :, None]
    )
    arrival_slot = jnp.sum(jnp.where(arrival_hit, local_slot[:, None, :], 0), axis=2).reshape(
        blocks_each
    )
    from_arrival = jnp.argmax(
        arrival_slot[None, :] == jnp.arange(blocks_each, dtype=jnp.int32)[:, None], axis=1
    )
    placed = jnp.take(incoming, from_arrival, axis=1)
    kv_pages = jnp.concatenate(
        [
            placed[..., head * head_dim : (head + 1) * head_dim]
            for head in range(kv_count)
            for _ in range(rep)
        ],
        axis=-1,
    )

    ffn_in = normalize(residual_all.astype(f32), ffn_gain).astype(bf16)
    gate_up = jnp.dot(
        ffn_in.reshape(-1, model_width), gateup_full, preferred_element_type=f32
    )
    hidden = (jax.nn.silu(gate_up[:, :unit_count]) * gate_up[:, unit_count:]).astype(bf16)
    kv_pages, hidden = lax.optimization_barrier((kv_pages, hidden))
    contract_last = (((1,), (1,)), ((), ()))
    if col_count == 2:
        other_w = lax.dynamic_slice_in_dim(down_full, (1 - col_index) * local_feat, local_feat, 0)
        own_w = lax.dynamic_slice_in_dim(down_full, col_index * local_feat, local_feat, 0)
        theirs = lax.dot_general(
            hidden, other_w, contract_last, preferred_element_type=f32
        ).astype(bf16)
        arrived = lax.ppermute(theirs, "col", [(0, 1), (1, 0)])
        mine = lax.dot_general(
            hidden, own_w, contract_last, preferred_element_type=f32
        ).astype(bf16)
        mine = lax.optimization_barrier(mine)
        ffn_sum = (mine.astype(f32) + arrived.astype(f32)).reshape(
            prompt_count, seq_len, local_feat
        )
    else:
        ffn_terms = lax.dot_general(
            hidden, down_full, contract_last, preferred_element_type=f32
        ).astype(bf16)
        ffn_sum = lax.psum_scatter(
            ffn_terms.reshape(prompt_count, seq_len, model_width),
            "col",
            scatter_dimension=2,
            tiled=True,
        ).astype(f32)
    layer_out = (residual.astype(f32) + ffn_sum).astype(bf16)
    return (layer_out, kv_pages)


def solution(mesh):
    in_specs = (
        P(("row", "page"), None, "col"),
        P(("row", "page")),
        P("row", None),
        P(("row", "page"), "col"),
        P(None, ("row", "page"), None),
        P("col", ("row", "page")),
        P(None, ("row", "page"), "col"),
        P("col", ("row", "page")),
        P(),
        P(),
        P(),
        P(),
    )
    out_specs = (P(("row", "page"), None, "col"), P(None, ("row", "page"), None, "col"))
    return jax.shard_map(
        on_device, mesh=mesh, in_specs=in_specs, out_specs=out_specs, check_vma=False
    )
```

```python
import jax
import jax.numpy as jnp
from jax import lax
from jax.experimental.layout import Layout, with_layout_constraint
from jax.sharding import PartitionSpec as P

PAGE_LEN = 128


def normalize(values, norm_gain):
    mean_sq = jnp.mean(values * values, axis=-1, keepdims=True)
    return values * lax.rsqrt(mean_sq + 1e-06) * norm_gain


def rotate(values):
    row_count = values.shape[-3]
    head_dim = values.shape[-1]
    half_dim = head_dim // 2
    frequency = 10000.0 ** (-2.0 * jnp.arange(half_dim, dtype=jnp.float32) / head_dim)
    angles = jnp.arange(row_count, dtype=jnp.float32)[:, None] * frequency[None, :]
    cosine = jnp.cos(angles)[:, None, :]
    sine_table = jnp.sin(angles)[:, None, :]
    leading = values[..., :half_dim]
    trailing = values[..., half_dim:]
    return jnp.concatenate(
        [leading * cosine - trailing * sine_table, trailing * cosine + leading * sine_table],
        axis=-1,
    )


def attend(query_rows, key_rows, value_rows, length):
    kv_count, row_count, group, head_dim = query_rows.shape
    scores = jnp.einsum(
        "gqre,gke->grqk", query_rows, key_rows, preferred_element_type=jnp.float32
    ) * head_dim ** (-0.5)
    positions = jnp.arange(row_count, dtype=jnp.int32)
    seen_keys = (positions[None, :] <= positions[:, None]) & (positions[None, :] < length)
    exp_scores = jnp.where(seen_keys, jnp.exp(scores), 0.0)
    attn_probs = (exp_scores / jnp.sum(exp_scores, axis=-1, keepdims=True)).astype(jnp.bfloat16)
    attended = jnp.einsum(
        "grqk,gke->qgre", attn_probs, value_rows, preferred_element_type=jnp.float32
    )
    live_rows = (positions < length)[:, None, None, None]
    return jnp.where(live_rows, attended, 0.0).astype(jnp.bfloat16)


def gather_col(values, col_count, col_index):
    if col_count != 2:
        return lax.all_gather(values, "col", axis=values.ndim - 1, tiled=True)
    other = lax.ppermute(values, "col", [(0, 1), (1, 0)])
    first = jnp.where(col_index == 0, values, other)
    second = jnp.where(col_index == 0, other, values)
    return jnp.concatenate([first, second], axis=-1)


def gather_rows(piece):
    rows_major = Layout(major_to_minor=(0, 1))
    piece = with_layout_constraint(piece, rows_major)
    full = lax.all_gather(piece, ("row", "page"), axis=0, tiled=True)
    return with_layout_constraint(full, rows_major)


def on_device(
    tokens,
    lengths,
    page_slot,
    w_query,
    w_keyval,
    w_out,
    w_gateup,
    w_down,
    attn_gain,
    ffn_gain,
    query_gain,
    key_gain,
):
    bf16 = jnp.bfloat16
    f32 = jnp.float32
    col_count = lax.axis_size("col")
    col_index = lax.axis_index("col")
    head_dim = query_gain.shape[0]
    local_width = w_query.shape[1]
    local_heads = local_width // head_dim
    kv_heads = w_keyval.shape[2] // head_dim
    group_size = local_heads * col_count // kv_heads
    kv_count = max(1, local_heads // group_size)
    rep = local_heads // kv_count
    kv_width = kv_count * head_dim
    kv_start = (col_index * local_heads // group_size) * head_dim
    prompt_count, seq_len, local_feat = tokens.shape
    model_width = attn_gain.shape[0]
    unit_count = w_gateup.shape[2]

    gathered = gather_col(tokens, col_count, col_index)

    keyval_piece = lax.dynamic_slice_in_dim(w_keyval, kv_start, kv_width, axis=2)
    attn_piece = jnp.concatenate(
        [w_query, keyval_piece[0], keyval_piece[1], w_out.T], axis=1
    ).astype(bf16)
    ffn_piece = jnp.concatenate([w_gateup[0], w_gateup[1], w_down.T], axis=1).astype(bf16)
    attn_full = gather_rows(attn_piece)
    ffn_full = gather_rows(ffn_piece)
    gateup_full = ffn_full[:, : 2 * unit_count]
    down_full = ffn_full[:, 2 * unit_count :]
    qkv_width = local_width + 2 * kv_width
    out_t = attn_full[:, qkv_width:]

    attn_in = normalize(gathered.astype(f32), attn_gain).astype(bf16)
    projected = jnp.dot(
        attn_in.reshape(-1, model_width), attn_full[:, :qkv_width], preferred_element_type=f32
    ).reshape(prompt_count, seq_len, qkv_width)
    heads = projected[:, :, : local_width + kv_width].reshape(
        prompt_count, seq_len, local_heads + kv_count, head_dim
    )
    gains = jnp.concatenate(
        [
            jnp.broadcast_to(query_gain, (local_heads, head_dim)),
            jnp.broadcast_to(key_gain, (kv_count, head_dim)),
        ]
    )
    rotated = rotate(normalize(heads, gains)).astype(bf16)
    values_in = projected[:, :, local_width + kv_width :].astype(bf16)
    keys_rot = rotated[:, :, local_heads:]
    parts = []
    for prompt in range(prompt_count):
        query_rows = rotated[prompt, :, :local_heads].reshape(seq_len, kv_count, rep, head_dim)
        parts.append(
            attend(
                query_rows.transpose(1, 0, 2, 3),
                keys_rot[prompt].transpose(1, 0, 2),
                values_in[prompt].reshape(seq_len, kv_count, head_dim).transpose(1, 0, 2),
                lengths[prompt],
            ).reshape(seq_len, local_width)
        )
    attended = jnp.stack(parts).reshape(-1, local_width)
    attn_terms = lax.dot_general(
        attended, out_t, (((1,), (1,)), ((), ())), preferred_element_type=f32
    ).astype(bf16).reshape(prompt_count, seq_len, model_width)

    if col_count == 2:
        attn_other = lax.ppermute(attn_terms, "col", [(0, 1), (1, 0)])
        attn_sum = attn_terms.astype(f32) + attn_other.astype(f32)
        residual_all = (gathered.astype(f32) + attn_sum).astype(bf16)
        residual = lax.dynamic_slice_in_dim(
            residual_all, col_index * local_feat, local_feat, axis=2
        )
    else:
        attn_sum = lax.psum_scatter(attn_terms, "col", scatter_dimension=2, tiled=True)
        residual = (tokens.astype(f32) + attn_sum.astype(f32)).astype(bf16)
        residual_all = lax.all_gather(residual, "col", axis=2, tiled=True)

    page_count = lax.axis_size("page")
    page_index = lax.axis_index("page")
    blocks_each = prompt_count * (seq_len // PAGE_LEN)
    capacity = blocks_each // page_count
    owners = page_slot // blocks_each
    local_slot = page_slot % blocks_each
    owners = owners.reshape(page_count, blocks_each)
    local_slot = local_slot.reshape(page_count, blocks_each)
    same_owner = owners[:, :, None] == owners[:, None, :]
    earlier = (
        jnp.arange(blocks_each, dtype=jnp.int32)[None, :]
        < jnp.arange(blocks_each, dtype=jnp.int32)[:, None]
    )
    order_in = jnp.sum((same_owner & earlier[None]).astype(jnp.int32), axis=2)
    my_owners = lax.dynamic_index_in_dim(owners, page_index, 0, keepdims=False)
    my_order = lax.dynamic_index_in_dim(order_in, page_index, 0, keepdims=False)
    send_pos = my_owners * capacity + my_order
    live_rows = (jnp.arange(seq_len, dtype=jnp.int32)[None, :] < lengths[:, None])[:, :, None]
    keys_flat = keys_rot.reshape(prompt_count, seq_len, kv_width)
    both = jnp.stack([keys_flat, values_in])
    both = jnp.where(live_rows[None], both, jnp.zeros_like(both)).reshape(
        2, blocks_each, PAGE_LEN, kv_width
    )
    from_block = jnp.argmax(
        send_pos[None, :] == jnp.arange(blocks_each, dtype=jnp.int32)[:, None], axis=1
    )
    outgoing = jnp.take(both, from_block, axis=1)
    incoming = lax.all_to_all(outgoing, "page", split_axis=1, concat_axis=1, tiled=True)
    arrival_hit = (owners[:, None, :] == page_index) & (
        order_in[:, None, :] == jnp.arange(capacity, dtype=jnp.int32)[None, :, None]
    )
    arrival_slot = jnp.sum(jnp.where(arrival_hit, local_slot[:, None, :], 0), axis=2).reshape(
        blocks_each
    )
    from_arrival = jnp.argmax(
        arrival_slot[None, :] == jnp.arange(blocks_each, dtype=jnp.int32)[:, None], axis=1
    )
    placed = jnp.take(incoming, from_arrival, axis=1)
    kv_pages = jnp.concatenate(
        [
            placed[..., head * head_dim : (head + 1) * head_dim]
            for head in range(kv_count)
            for _ in range(rep)
        ],
        axis=-1,
    )

    ffn_in = normalize(residual_all.astype(f32), ffn_gain).astype(bf16)
    ffn_in = ffn_in.reshape(-1, model_width)
    kv_pages, ffn_in = lax.optimization_barrier((kv_pages, ffn_in))
    contract_last = (((1,), (1,)), ((), ()))

    def hidden_of(rows):
        gate_up = jnp.dot(rows, gateup_full, preferred_element_type=f32)
        return (jax.nn.silu(gate_up[:, :unit_count]) * gate_up[:, unit_count:]).astype(bf16)

    def down_terms(hidden, weights):
        return lax.dot_general(
            hidden, weights, contract_last, preferred_element_type=f32
        ).astype(bf16)

    if col_count == 2:
        other_w = lax.dynamic_slice_in_dim(down_full, (1 - col_index) * local_feat, local_feat, 0)
        own_w = lax.dynamic_slice_in_dim(down_full, col_index * local_feat, local_feat, 0)
        first_in, second_in = jnp.split(ffn_in, 2)
        first_hidden = hidden_of(first_in)
        first_theirs = down_terms(first_hidden, other_w)
        first_arrived = lax.ppermute(first_theirs, "col", [(0, 1), (1, 0)])
        second_in, first_theirs = lax.optimization_barrier((second_in, first_theirs))
        second_hidden = hidden_of(second_in)
        second_theirs = down_terms(second_hidden, other_w)
        second_arrived = lax.ppermute(second_theirs, "col", [(0, 1), (1, 0)])
        hidden = jnp.concatenate([first_hidden, second_hidden])
        hidden, second_theirs = lax.optimization_barrier((hidden, second_theirs))
        mine = lax.optimization_barrier(down_terms(hidden, own_w))
        arrived = jnp.concatenate([first_arrived, second_arrived])
        ffn_sum = (mine.astype(f32) + arrived.astype(f32)).reshape(
            prompt_count, seq_len, local_feat
        )
    else:
        ffn_terms = down_terms(hidden_of(ffn_in), down_full)
        ffn_sum = lax.psum_scatter(
            ffn_terms.reshape(prompt_count, seq_len, model_width),
            "col",
            scatter_dimension=2,
            tiled=True,
        ).astype(f32)
    layer_out = (residual.astype(f32) + ffn_sum).astype(bf16)
    return (layer_out, kv_pages)


def solution(mesh):
    in_specs = (
        P(("row", "page"), None, "col"),
        P(("row", "page")),
        P("row", None),
        P(("row", "page"), "col"),
        P(None, ("row", "page"), None),
        P("col", ("row", "page")),
        P(None, ("row", "page"), "col"),
        P("col", ("row", "page")),
        P(),
        P(),
        P(),
        P(),
    )
    out_specs = (P(("row", "page"), None, "col"), P(None, ("row", "page"), None, "col"))
    return jax.shard_map(
        on_device, mesh=mesh, in_specs=in_specs, out_specs=out_specs, check_vma=False
    )
```

```python
import jax
import jax.numpy as jnp
from jax import lax
from jax.experimental.layout import Layout, with_layout_constraint
from jax.sharding import PartitionSpec as P

PAGE_LEN = 128


def normalize(values, norm_gain):
    mean_sq = jnp.mean(values * values, axis=-1, keepdims=True)
    return values * lax.rsqrt(mean_sq + 1e-06) * norm_gain


def rotate(values):
    row_count = values.shape[-3]
    head_dim = values.shape[-1]
    half_dim = head_dim // 2
    frequency = 10000.0 ** (-2.0 * jnp.arange(half_dim, dtype=jnp.float32) / head_dim)
    angles = jnp.arange(row_count, dtype=jnp.float32)[:, None] * frequency[None, :]
    cosine = jnp.cos(angles)[:, None, :]
    sine_table = jnp.sin(angles)[:, None, :]
    leading = values[..., :half_dim]
    trailing = values[..., half_dim:]
    return jnp.concatenate(
        [leading * cosine - trailing * sine_table, trailing * cosine + leading * sine_table],
        axis=-1,
    )


def attend(query_rows, key_rows, value_rows, length):
    kv_count, row_count, group, head_dim = query_rows.shape
    scores = jnp.einsum(
        "gqre,gke->grqk", query_rows, key_rows, preferred_element_type=jnp.float32
    ) * head_dim ** (-0.5)
    positions = jnp.arange(row_count, dtype=jnp.int32)
    seen_keys = (positions[None, :] <= positions[:, None]) & (positions[None, :] < length)
    exp_scores = jnp.where(seen_keys, jnp.exp(scores), 0.0)
    attn_probs = (exp_scores / jnp.sum(exp_scores, axis=-1, keepdims=True)).astype(jnp.bfloat16)
    attended = jnp.einsum(
        "grqk,gke->qgre", attn_probs, value_rows, preferred_element_type=jnp.float32
    )
    live_rows = (positions < length)[:, None, None, None]
    return jnp.where(live_rows, attended, 0.0).astype(jnp.bfloat16)


def gather_col(values, col_count, col_index):
    if col_count != 2:
        return lax.all_gather(values, "col", axis=values.ndim - 1, tiled=True)
    other = lax.ppermute(values, "col", [(0, 1), (1, 0)])
    first = jnp.where(col_index == 0, values, other)
    second = jnp.where(col_index == 0, other, values)
    return jnp.concatenate([first, second], axis=-1)


def gather_rows(piece):
    rows_major = Layout(major_to_minor=(0, 1))
    piece = with_layout_constraint(piece, rows_major)
    full = lax.all_gather(piece, ("row", "page"), axis=0, tiled=True)
    return with_layout_constraint(full, rows_major)


def exchange(values, axis, bit):
    count = lax.axis_size(axis)
    return lax.ppermute(values, axis, [(i, i ^ bit) for i in range(count)])


def gather_doubling(piece):
    row_count = lax.axis_size("row")
    page_count = lax.axis_size("page")
    if row_count & (row_count - 1) or page_count & (page_count - 1):
        return gather_rows(piece)
    held = piece[None]
    bit = 1
    while bit < page_count:
        other = exchange(held, "page", bit)
        upper = (lax.axis_index("page") & bit) != 0
        held = jnp.concatenate(
            [jnp.where(upper, other, held), jnp.where(upper, held, other)], axis=0
        )
        bit *= 2
    held = held[None]
    bit = row_count // 2
    while bit >= 1:
        other = exchange(held, "row", bit)
        upper = (lax.axis_index("row") & bit) != 0
        held = jnp.stack(
            [jnp.where(upper, other, held), jnp.where(upper, held, other)], axis=1
        ).reshape(2 * held.shape[0], *held.shape[1:])
        bit //= 2
    return held.reshape(-1, piece.shape[1])


def on_device(
    tokens,
    lengths,
    page_slot,
    w_query,
    w_keyval,
    w_out,
    w_gateup,
    w_down,
    attn_gain,
    ffn_gain,
    query_gain,
    key_gain,
):
    bf16 = jnp.bfloat16
    f32 = jnp.float32
    col_count = lax.axis_size("col")
    col_index = lax.axis_index("col")
    head_dim = query_gain.shape[0]
    local_width = w_query.shape[1]
    local_heads = local_width // head_dim
    kv_heads = w_keyval.shape[2] // head_dim
    group_size = local_heads * col_count // kv_heads
    kv_count = max(1, local_heads // group_size)
    rep = local_heads // kv_count
    kv_width = kv_count * head_dim
    kv_start = (col_index * local_heads // group_size) * head_dim
    prompt_count, seq_len, local_feat = tokens.shape
    model_width = attn_gain.shape[0]
    unit_count = w_gateup.shape[2]

    gathered = gather_col(tokens, col_count, col_index)

    keyval_piece = lax.dynamic_slice_in_dim(w_keyval, kv_start, kv_width, axis=2)
    attn_piece = jnp.concatenate(
        [w_query, keyval_piece[0], keyval_piece[1], w_out.T], axis=1
    ).astype(bf16)
    ffn_piece = jnp.concatenate([w_gateup[0], w_gateup[1], w_down.T], axis=1).astype(bf16)
    ffn_full = gather_rows(ffn_piece)
    attn_full = gather_doubling(attn_piece)
    gateup_full = ffn_full[:, : 2 * unit_count]
    qkv_width = local_width + 2 * kv_width
    out_t = attn_full[:, qkv_width:]

    attn_in = normalize(gathered.astype(f32), attn_gain).astype(bf16)
    projected = jnp.dot(
        attn_in.reshape(-1, model_width), attn_full[:, :qkv_width], preferred_element_type=f32
    ).reshape(prompt_count, seq_len, qkv_width)
    heads = projected[:, :, : local_width + kv_width].reshape(
        prompt_count, seq_len, local_heads + kv_count, head_dim
    )
    gains = jnp.concatenate(
        [
            jnp.broadcast_to(query_gain, (local_heads, head_dim)),
            jnp.broadcast_to(key_gain, (kv_count, head_dim)),
        ]
    )
    rotated = rotate(normalize(heads, gains)).astype(bf16)
    values_in = projected[:, :, local_width + kv_width :].astype(bf16)
    keys_rot = rotated[:, :, local_heads:]
    parts = []
    for prompt in range(prompt_count):
        query_rows = rotated[prompt, :, :local_heads].reshape(seq_len, kv_count, rep, head_dim)
        parts.append(
            attend(
                query_rows.transpose(1, 0, 2, 3),
                keys_rot[prompt].transpose(1, 0, 2),
                values_in[prompt].reshape(seq_len, kv_count, head_dim).transpose(1, 0, 2),
                lengths[prompt],
            ).reshape(seq_len, local_width)
        )
    attended = jnp.stack(parts).reshape(-1, local_width)
    attn_terms = lax.dot_general(
        attended, out_t, (((1,), (1,)), ((), ())), preferred_element_type=f32
    ).astype(bf16).reshape(prompt_count, seq_len, model_width)

    if col_count == 2:
        attn_other = lax.ppermute(attn_terms, "col", [(0, 1), (1, 0)])
        attn_sum = attn_terms.astype(f32) + attn_other.astype(f32)
        residual_all = (gathered.astype(f32) + attn_sum).astype(bf16)
        residual = lax.dynamic_slice_in_dim(
            residual_all, col_index * local_feat, local_feat, axis=2
        )
    else:
        attn_sum = lax.psum_scatter(attn_terms, "col", scatter_dimension=2, tiled=True)
        residual = (tokens.astype(f32) + attn_sum.astype(f32)).astype(bf16)
        residual_all = lax.all_gather(residual, "col", axis=2, tiled=True)

    page_count = lax.axis_size("page")
    page_index = lax.axis_index("page")
    blocks_each = prompt_count * (seq_len // PAGE_LEN)
    capacity = blocks_each // page_count
    owners = page_slot // blocks_each
    local_slot = page_slot % blocks_each
    owners = owners.reshape(page_count, blocks_each)
    local_slot = local_slot.reshape(page_count, blocks_each)
    same_owner = owners[:, :, None] == owners[:, None, :]
    earlier = (
        jnp.arange(blocks_each, dtype=jnp.int32)[None, :]
        < jnp.arange(blocks_each, dtype=jnp.int32)[:, None]
    )
    order_in = jnp.sum((same_owner & earlier[None]).astype(jnp.int32), axis=2)
    my_owners = lax.dynamic_index_in_dim(owners, page_index, 0, keepdims=False)
    my_order = lax.dynamic_index_in_dim(order_in, page_index, 0, keepdims=False)
    send_pos = my_owners * capacity + my_order
    live_rows = (jnp.arange(seq_len, dtype=jnp.int32)[None, :] < lengths[:, None])[:, :, None]
    keys_flat = keys_rot.reshape(prompt_count, seq_len, kv_width)
    both = jnp.stack([keys_flat, values_in])
    both = jnp.where(live_rows[None], both, jnp.zeros_like(both)).reshape(
        2, blocks_each, PAGE_LEN, kv_width
    )
    from_block = jnp.argmax(
        send_pos[None, :] == jnp.arange(blocks_each, dtype=jnp.int32)[:, None], axis=1
    )
    outgoing = jnp.take(both, from_block, axis=1)
    incoming = lax.all_to_all(outgoing, "page", split_axis=1, concat_axis=1, tiled=True)
    arrival_hit = (owners[:, None, :] == page_index) & (
        order_in[:, None, :] == jnp.arange(capacity, dtype=jnp.int32)[None, :, None]
    )
    arrival_slot = jnp.sum(jnp.where(arrival_hit, local_slot[:, None, :], 0), axis=2).reshape(
        blocks_each
    )
    from_arrival = jnp.argmax(
        arrival_slot[None, :] == jnp.arange(blocks_each, dtype=jnp.int32)[:, None], axis=1
    )
    placed = jnp.take(incoming, from_arrival, axis=1)
    kv_pages = jnp.concatenate(
        [
            placed[..., head * head_dim : (head + 1) * head_dim]
            for head in range(kv_count)
            for _ in range(rep)
        ],
        axis=-1,
    )

    ffn_in = normalize(residual_all.astype(f32), ffn_gain).astype(bf16)
    ffn_in = ffn_in.reshape(-1, model_width)
    kv_pages, ffn_in = lax.optimization_barrier((kv_pages, ffn_in))
    contract_last = (((1,), (1,)), ((), ()))

    def hidden_of(rows):
        gate_up = jnp.dot(rows, gateup_full, preferred_element_type=f32)
        return (jax.nn.silu(gate_up[:, :unit_count]) * gate_up[:, unit_count:]).astype(bf16)

    def down_terms(hidden, weights):
        return lax.dot_general(
            hidden, weights, contract_last, preferred_element_type=f32
        ).astype(bf16)

    if col_count == 2:
        down_at = lambda col: lax.dynamic_slice(
            ffn_full, (col * local_feat, 2 * unit_count), (local_feat, unit_count)
        )
        hidden = hidden_of(ffn_in)
        theirs = down_terms(hidden, down_at(1 - col_index))
        arrived = lax.ppermute(theirs, "col", [(0, 1), (1, 0)])
        mine = lax.optimization_barrier(down_terms(hidden, down_at(col_index)))
        ffn_sum = (mine.astype(f32) + arrived.astype(f32)).reshape(
            prompt_count, seq_len, local_feat
        )
    else:
        ffn_terms = down_terms(hidden_of(ffn_in), ffn_full[:, 2 * unit_count :])
        ffn_sum = lax.psum_scatter(
            ffn_terms.reshape(prompt_count, seq_len, model_width),
            "col",
            scatter_dimension=2,
            tiled=True,
        ).astype(f32)
    layer_out = (residual.astype(f32) + ffn_sum).astype(bf16)
    return (layer_out, kv_pages)


def solution(mesh):
    in_specs = (
        P(("row", "page"), None, "col"),
        P(("row", "page")),
        P("row", None),
        P(("row", "page"), "col"),
        P(None, ("row", "page"), None),
        P("col", ("row", "page")),
        P(None, ("row", "page"), "col"),
        P("col", ("row", "page")),
        P(),
        P(),
        P(),
        P(),
    )
    out_specs = (P(("row", "page"), None, "col"), P(None, ("row", "page"), None, "col"))
    return jax.shard_map(
        on_device, mesh=mesh, in_specs=in_specs, out_specs=out_specs, check_vma=False
    )
```

```python
import jax
import jax.numpy as jnp
from jax import lax
from jax.experimental.layout import Layout, with_layout_constraint
from jax.sharding import PartitionSpec as P

PAGE_LEN = 128


def normalize(values, norm_gain):
    mean_sq = jnp.mean(values * values, axis=-1, keepdims=True)
    return values * lax.rsqrt(mean_sq + 1e-06) * norm_gain


def rotate(values):
    row_count = values.shape[-3]
    head_dim = values.shape[-1]
    half_dim = head_dim // 2
    frequency = 10000.0 ** (-2.0 * jnp.arange(half_dim, dtype=jnp.float32) / head_dim)
    angles = jnp.arange(row_count, dtype=jnp.float32)[:, None] * frequency[None, :]
    cosine = jnp.cos(angles)[:, None, :]
    sine_table = jnp.sin(angles)[:, None, :]
    leading = values[..., :half_dim]
    trailing = values[..., half_dim:]
    return jnp.concatenate(
        [leading * cosine - trailing * sine_table, trailing * cosine + leading * sine_table],
        axis=-1,
    )


def attend(query_rows, key_rows, value_rows, length):
    kv_count, row_count, group, head_dim = query_rows.shape
    scores = jnp.einsum(
        "gqre,gke->grqk", query_rows, key_rows, preferred_element_type=jnp.float32
    ) * head_dim ** (-0.5)
    positions = jnp.arange(row_count, dtype=jnp.int32)
    seen_keys = (positions[None, :] <= positions[:, None]) & (positions[None, :] < length)
    exp_scores = jnp.where(seen_keys, jnp.exp(scores), 0.0)
    attn_probs = (exp_scores / jnp.sum(exp_scores, axis=-1, keepdims=True)).astype(jnp.bfloat16)
    attended = jnp.einsum(
        "grqk,gke->qgre", attn_probs, value_rows, preferred_element_type=jnp.float32
    )
    live_rows = (positions < length)[:, None, None, None]
    return jnp.where(live_rows, attended, 0.0).astype(jnp.bfloat16)


def gather_col(values, col_count, col_index):
    if col_count != 2:
        return lax.all_gather(values, "col", axis=values.ndim - 1, tiled=True)
    other = lax.ppermute(values, "col", [(0, 1), (1, 0)])
    first = jnp.where(col_index == 0, values, other)
    second = jnp.where(col_index == 0, other, values)
    return jnp.concatenate([first, second], axis=-1)


def gather_rows(piece):
    rows_major = Layout(major_to_minor=(0, 1))
    piece = with_layout_constraint(piece, rows_major)
    full = lax.all_gather(piece, ("row", "page"), axis=0, tiled=True)
    return with_layout_constraint(full, rows_major)


def exchange(values, axis, bit):
    count = lax.axis_size(axis)
    return lax.ppermute(values, axis, [(i, i ^ bit) for i in range(count)])


def gather_doubling(piece, gathered):
    row_count = lax.axis_size("row")
    page_count = lax.axis_size("page")
    if row_count & (row_count - 1) or page_count & (page_count - 1):
        return gather_rows(piece), gathered
    held = piece[None]
    bit = 1
    while bit < page_count:
        other = exchange(held, "page", bit)
        upper = (lax.axis_index("page") & bit) != 0
        held = jnp.concatenate(
            [jnp.where(upper, other, held), jnp.where(upper, held, other)], axis=0
        )
        bit *= 2
    held, gathered = lax.optimization_barrier((held, gathered))
    held = held[None]
    bit = row_count // 2
    while bit >= 1:
        other = exchange(held, "row", bit)
        upper = (lax.axis_index("row") & bit) != 0
        held = jnp.stack(
            [jnp.where(upper, other, held), jnp.where(upper, held, other)], axis=1
        ).reshape(2 * held.shape[0], *held.shape[1:])
        bit //= 2
    return held.reshape(-1, piece.shape[1]), gathered


def on_device(
    tokens,
    lengths,
    page_slot,
    w_query,
    w_keyval,
    w_out,
    w_gateup,
    w_down,
    attn_gain,
    ffn_gain,
    query_gain,
    key_gain,
):
    bf16 = jnp.bfloat16
    f32 = jnp.float32
    col_count = lax.axis_size("col")
    col_index = lax.axis_index("col")
    head_dim = query_gain.shape[0]
    local_width = w_query.shape[1]
    local_heads = local_width // head_dim
    kv_heads = w_keyval.shape[2] // head_dim
    group_size = local_heads * col_count // kv_heads
    kv_count = max(1, local_heads // group_size)
    rep = local_heads // kv_count
    kv_width = kv_count * head_dim
    kv_start = (col_index * local_heads // group_size) * head_dim
    prompt_count, seq_len, local_feat = tokens.shape
    model_width = attn_gain.shape[0]
    unit_count = w_gateup.shape[2]

    gathered = gather_col(tokens, col_count, col_index)

    keyval_piece = lax.dynamic_slice_in_dim(w_keyval, kv_start, kv_width, axis=2)
    attn_piece = jnp.concatenate(
        [w_query, keyval_piece[0], keyval_piece[1], w_out.T], axis=1
    ).astype(bf16)
    ffn_piece = jnp.concatenate([w_gateup[0], w_gateup[1], w_down.T], axis=1).astype(bf16)
    ffn_full = gather_rows(ffn_piece)
    attn_full, gathered = gather_doubling(attn_piece, gathered)
    gateup_full = ffn_full[:, : 2 * unit_count]
    qkv_width = local_width + 2 * kv_width
    out_t = attn_full[:, qkv_width:]

    attn_in = normalize(gathered.astype(f32), attn_gain).astype(bf16)
    projected = jnp.dot(
        attn_in.reshape(-1, model_width), attn_full[:, :qkv_width], preferred_element_type=f32
    ).reshape(prompt_count, seq_len, qkv_width)
    heads = projected[:, :, : local_width + kv_width].reshape(
        prompt_count, seq_len, local_heads + kv_count, head_dim
    )
    gains = jnp.concatenate(
        [
            jnp.broadcast_to(query_gain, (local_heads, head_dim)),
            jnp.broadcast_to(key_gain, (kv_count, head_dim)),
        ]
    )
    rotated = rotate(normalize(heads, gains)).astype(bf16)
    values_in = projected[:, :, local_width + kv_width :].astype(bf16)
    keys_rot = rotated[:, :, local_heads:]
    parts = []
    for prompt in range(prompt_count):
        query_rows = rotated[prompt, :, :local_heads].reshape(seq_len, kv_count, rep, head_dim)
        parts.append(
            attend(
                query_rows.transpose(1, 0, 2, 3),
                keys_rot[prompt].transpose(1, 0, 2),
                values_in[prompt].reshape(seq_len, kv_count, head_dim).transpose(1, 0, 2),
                lengths[prompt],
            ).reshape(seq_len, local_width)
        )
    attended = jnp.stack(parts).reshape(-1, local_width)
    attn_terms = lax.dot_general(
        attended, out_t, (((1,), (1,)), ((), ())), preferred_element_type=f32
    ).astype(bf16).reshape(prompt_count, seq_len, model_width)

    if col_count == 2:
        attn_other = lax.ppermute(attn_terms, "col", [(0, 1), (1, 0)])
        attn_sum = attn_terms.astype(f32) + attn_other.astype(f32)
        residual_all = (gathered.astype(f32) + attn_sum).astype(bf16)
        residual = lax.dynamic_slice_in_dim(
            residual_all, col_index * local_feat, local_feat, axis=2
        )
    else:
        attn_sum = lax.psum_scatter(attn_terms, "col", scatter_dimension=2, tiled=True)
        residual = (tokens.astype(f32) + attn_sum.astype(f32)).astype(bf16)
        residual_all = lax.all_gather(residual, "col", axis=2, tiled=True)

    page_count = lax.axis_size("page")
    page_index = lax.axis_index("page")
    blocks_each = prompt_count * (seq_len // PAGE_LEN)
    capacity = blocks_each // page_count
    owners = page_slot // blocks_each
    local_slot = page_slot % blocks_each
    owners = owners.reshape(page_count, blocks_each)
    local_slot = local_slot.reshape(page_count, blocks_each)
    same_owner = owners[:, :, None] == owners[:, None, :]
    earlier = (
        jnp.arange(blocks_each, dtype=jnp.int32)[None, :]
        < jnp.arange(blocks_each, dtype=jnp.int32)[:, None]
    )
    order_in = jnp.sum((same_owner & earlier[None]).astype(jnp.int32), axis=2)
    my_owners = lax.dynamic_index_in_dim(owners, page_index, 0, keepdims=False)
    my_order = lax.dynamic_index_in_dim(order_in, page_index, 0, keepdims=False)
    send_pos = my_owners * capacity + my_order
    live_rows = (jnp.arange(seq_len, dtype=jnp.int32)[None, :] < lengths[:, None])[:, :, None]
    keys_flat = keys_rot.reshape(prompt_count, seq_len, kv_width)
    both = jnp.stack([keys_flat, values_in])
    both = jnp.where(live_rows[None], both, jnp.zeros_like(both)).reshape(
        2, blocks_each, PAGE_LEN, kv_width
    )
    from_block = jnp.argmax(
        send_pos[None, :] == jnp.arange(blocks_each, dtype=jnp.int32)[:, None], axis=1
    )
    outgoing = jnp.take(both, from_block, axis=1)
    incoming = lax.all_to_all(outgoing, "page", split_axis=1, concat_axis=1, tiled=True)
    arrival_hit = (owners[:, None, :] == page_index) & (
        order_in[:, None, :] == jnp.arange(capacity, dtype=jnp.int32)[None, :, None]
    )
    arrival_slot = jnp.sum(jnp.where(arrival_hit, local_slot[:, None, :], 0), axis=2).reshape(
        blocks_each
    )
    from_arrival = jnp.argmax(
        arrival_slot[None, :] == jnp.arange(blocks_each, dtype=jnp.int32)[:, None], axis=1
    )
    placed = jnp.take(incoming, from_arrival, axis=1)
    kv_pages = jnp.concatenate(
        [
            placed[..., head * head_dim : (head + 1) * head_dim]
            for head in range(kv_count)
            for _ in range(rep)
        ],
        axis=-1,
    )

    ffn_in = normalize(residual_all.astype(f32), ffn_gain).astype(bf16)
    ffn_in = ffn_in.reshape(-1, model_width)
    kv_pages, ffn_in = lax.optimization_barrier((kv_pages, ffn_in))
    contract_last = (((1,), (1,)), ((), ()))

    def hidden_of(rows):
        gate_up = jnp.dot(rows, gateup_full, preferred_element_type=f32)
        return (jax.nn.silu(gate_up[:, :unit_count]) * gate_up[:, unit_count:]).astype(bf16)

    def down_terms(hidden, weights):
        return lax.dot_general(
            hidden, weights, contract_last, preferred_element_type=f32
        ).astype(bf16)

    if col_count == 2:
        def down_at(first, width):
            return lax.dynamic_slice(ffn_full, (first, 2 * unit_count), (width, unit_count))

        hidden = hidden_of(ffn_in)
        half = local_feat // 2
        other_first = (1 - col_index) * local_feat
        arrivals = []
        for first in (other_first, other_first + half):
            theirs = down_terms(hidden, down_at(first, half))
            arrivals.append(lax.ppermute(theirs, "col", [(0, 1), (1, 0)]))
        arrived = jnp.concatenate(arrivals, axis=1)
        mine = lax.optimization_barrier(down_terms(hidden, down_at(col_index * local_feat, local_feat)))
        ffn_sum = (mine.astype(f32) + arrived.astype(f32)).reshape(
            prompt_count, seq_len, local_feat
        )
    else:
        ffn_terms = down_terms(hidden_of(ffn_in), ffn_full[:, 2 * unit_count :])
        ffn_sum = lax.psum_scatter(
            ffn_terms.reshape(prompt_count, seq_len, model_width),
            "col",
            scatter_dimension=2,
            tiled=True,
        ).astype(f32)
    layer_out = (residual.astype(f32) + ffn_sum).astype(bf16)
    return (layer_out, kv_pages)


def solution(mesh):
    in_specs = (
        P(("row", "page"), None, "col"),
        P(("row", "page")),
        P("row", None),
        P(("row", "page"), "col"),
        P(None, ("row", "page"), None),
        P("col", ("row", "page")),
        P(None, ("row", "page"), "col"),
        P("col", ("row", "page")),
        P(),
        P(),
        P(),
        P(),
    )
    out_specs = (P(("row", "page"), None, "col"), P(None, ("row", "page"), None, "col"))
    return jax.shard_map(
        on_device, mesh=mesh, in_specs=in_specs, out_specs=out_specs, check_vma=False
    )
```
